128 devices in a mesh: narrow: 8 (over z_lo, x), wide: 16 (over z_hi, y, core).
Axes of the slice: x: 4, y: 4, z: 4 (z_hi: 2, z_lo: 2; z = z_hi * 2 + z_lo), core: 2. Of those that a mesh axis runs over, the one named last changes fastest.
Arguments:
- source: float32 [262144, 128], P(('narrow', 'wide')), may hold values from -6 to 6
- interp_maps: float32 [18, 2, 2, 128, 128], replicated, may hold values from -0.375 to 0.375
- phases: float32 [18, 262144, 64], P(None, ('narrow', 'wide')), may hold values from -3.140625 to 3.140625
Outputs:
- targets: float32 [262144, 128], P(('narrow', 'wide'))
The draws below stay inside these ranges and needn't reach their ends.
All inputs are finite; a program needn't handle non-finite values.
Results may differ from the reference program's by a relative error of at most 0.0003.
Values sent between devices are 32-bit elements; how exact they have to be, the bound alone decides.
No kernel may reach another device: no remote copies, remote signals or barrier semaphores. Data moves between devices by JAX's collectives and lax.ppermute only.
A program may use at most 128 MiB of HBM per device.

```python
import jax
import jax.numpy as jnp
from jax import lax

R = 64
BOX_DEV = 2048
LEVELS = 18
NBOX = 262144


def shard_levels(key, dims, shards, low, high):
    loudness = 1.0
    for axis_at, shards_of in shards:
        heights = jax.random.uniform(jax.random.fold_in(jax.random.fold_in(key, 6), axis_at), (shards_of,), jnp.float32, low / len(shards), high / len(shards))
        loudness = loudness * jnp.repeat(jnp.exp(heights), dims[axis_at] // shards_of).reshape((-1,) + (1,) * (len(dims) - 1 - axis_at))
    return loudness


def normal_values(stream_key, shape, scale, reach, split=(), dtype=jnp.bfloat16):
    level = shard_levels(stream_key, shape, split, -0.22, 0.18) if split else 1.0
    array = jax.random.normal(stream_key, shape, jnp.float32) * scale * level
    return jnp.minimum(jnp.maximum(array, -reach), reach).astype(dtype)


def setup_inputs(seed: int = 0) -> dict:
    splits = jax.random.split(jax.random.key(seed), 4)
    return {
        "source": normal_values(splits[0], (NBOX, 2 * R), 1.0, 6.0, ((0, 128),), jnp.float32),
        "interp_maps": normal_values(splits[1], (LEVELS, 2, 2, 2 * R, 2 * R), (4 * R) ** -0.5, 0.375, (), jnp.float32),
        "phases": jnp.clip(jax.random.uniform(splits[2], (LEVELS, NBOX, R), jnp.float32, -3.140625, 3.140625), -3.140625, 3.140625),
    }


HIGH = lax.Precision.HIGHEST


def rotate(values, angles):
    points = angles.shape[-1]
    real_part = values[..., :points]
    imag_part = values[..., points:]
    cosine = jnp.cos(angles)
    sine_part = jnp.sin(angles)
    return jnp.concatenate([cosine * real_part - sine_part * imag_part, sine_part * real_part + cosine * imag_part], axis=-1)


def multiply(values, matrix):
    return jnp.einsum("...k,kn->...n", values, matrix, precision=HIGH)


def pair_level(current, matrices, angles, bitpos):
    leading, boxes_all, columns = current.shape
    stride = 2 ** bitpos
    grouped = current.reshape(leading, boxes_all // (2 * stride), 2, stride, columns)
    low_half = grouped[:, :, 0]
    high_half = grouped[:, :, 1]
    even_out = multiply(low_half, matrices[0, 0]) + multiply(high_half, matrices[0, 1])
    odd_out = multiply(low_half, matrices[1, 0]) + multiply(high_half, matrices[1, 1])
    merged = jnp.stack([even_out, odd_out], axis=2).reshape(leading, boxes_all, columns)
    return rotate(merged, angles)


def reference(source, interp_maps, phases):
    current = source[None]
    for depth in range(LEVELS):
        current = pair_level(current, interp_maps[depth], phases[depth][None], depth)
    current = current[0].reshape(NBOX // BOX_DEV, BOX_DEV, 2 * R)
    return jnp.transpose(current, (1, 0, 2)).reshape(NBOX, 2 * R)
```

```python
import functools

import jax
import jax.numpy as jnp
from jax import lax
from jax.experimental import pallas as pl
from jax.experimental.pallas import tpu as pltpu
from jax.sharding import PartitionSpec as P

AXES = ("narrow", "wide")
SIN_HALF = (0.9999999957157406, -0.041666644924359314, 0.0005208156633383668, -3.095163447075199e-06, 1.0176428087056766e-08)
COS_HALF = (0.9999999532465265, -0.12499976265264102, 0.002603973680502671, -2.1646354078657635e-05, 9.044205735375736e-08)
CHUNK = 256
VMEM = 48 * 2**20


def horner(coefficients, z):
    total = jnp.full_like(z, coefficients[-1])
    for c in coefficients[-2::-1]:
        total = total * z + c
    return total


def cos_sin(x):
    z = x * x
    s = x * horner(SIN_HALF, z)
    c = horner(COS_HALF, z)
    return 1.0 - 0.5 * (s * s), s * c


def spread(cosine, sine, parity):
    left = lax.broadcasted_iota(jnp.int32, cosine.shape, 1) < 64
    c_roll = pltpu.roll(cosine, 64, 1)
    s_roll = pltpu.roll(sine, 64, 1)
    if parity == 0:
        return jnp.where(left, cosine, c_roll), jnp.where(left, -sine, s_roll)
    return jnp.where(left, c_roll, cosine), jnp.where(left, -s_roll, sine)


def rotate(values, cosine, sine, parity):
    c2, s2 = spread(cosine, sine, parity)
    return values * c2 + pltpu.roll(values, 64, 1) * s2


def dot3(x, w):
    k = x.shape[1]
    upper = x.astype(jnp.bfloat16)
    lower = (x - upper.astype(jnp.float32)).astype(jnp.bfloat16)
    w_up, w_low = w[:k], w[k:]
    dot = functools.partial(jnp.dot, preferred_element_type=jnp.float32)
    return dot(upper, w_up) + (dot(lower, w_up) + dot(upper, w_low))


def row_slices(stride, step, n=CHUNK):
    if stride >= n:
        per = stride // n
        return [pl.ds(pl.multiple_of((step // per) * 2 * stride + (step % per) * n, n), n)]
    base = step * 2 * n
    if stride >= 8:
        return [pl.ds(pl.multiple_of(base + j * 2 * stride, 8), stride) for j in range(n // stride)]
    return [pl.ds(base + o, n // stride, stride=2 * stride) for o in range(stride)]


def shifted(s, by):
    return pl.ds(s.start + by, s.size, stride=s.stride)


def load_pairs(ref, slices, stride):
    def cat(parts):
        return parts[0] if len(parts) == 1 else jnp.concatenate(parts, axis=0)

    return cat([ref[s, :] for s in slices]), cat([ref[shifted(s, stride), :] for s in slices])


def store_pairs(ref, slices, stride, low, high):
    at = 0
    for s in slices:
        ref[s, :] = low[at : at + s.size]
        ref[shifted(s, stride), :] = high[at : at + s.size]
        at += s.size


def pair_level(state, cosine, sine, w, stride, parity, put=None):
    rows = state.shape[0]

    def step(i, carry):
        slices = row_slices(stride, i)
        low, high = load_pairs(state, slices, stride)
        new = dot3(jnp.concatenate([low, high], axis=1), w)
        c_low, c_high = load_pairs(cosine, slices, stride)
        s_low, s_high = load_pairs(sine, slices, stride)
        low = rotate(new[:, :128], c_low, s_low, parity)
        high = rotate(new[:, 128:], c_high, s_high, parity)
        if put is None:
            store_pairs(state, slices, stride, low, high)
        else:
            put(i, low, high)
        return carry

    lax.fori_loop(0, rows // (2 * CHUNK), step, 0)


def pack_kernel(phases, out):
    columns = phases.shape[2]
    for j in range(columns // 128):
        block = jnp.concatenate([phases[0, :, pl.ds(j * 128, 128)], phases[1, :, pl.ds(j * 128, 128)]], axis=0)
        out[pl.ds(j * 8, 8)] = block.T.reshape(8, 16, 128)


def weights_kernel(maps, out):
    w = jnp.concatenate(
        [jnp.concatenate([maps[0, 0, 0], maps[0, 1, 0]], axis=1), jnp.concatenate([maps[0, 0, 1], maps[0, 1, 1]], axis=1)],
        axis=0,
    )
    upper = w.astype(jnp.bfloat16)
    out[0, :256] = upper
    out[0, 256:] = (w - upper.astype(jnp.float32)).astype(jnp.bfloat16)


def local_kernel(levels, source, phases, weights, state, cosine, sine):
    pair = pl.program_id(0)

    @pl.when(pair == 0)
    def _():
        state[...] = source[...]

    def angles(j, carry):
        at = pl.ds(pl.multiple_of(j * 128, 128), 128)
        block = jnp.concatenate([phases[0, :, at], phases[1, :, at]], axis=0)
        c, s = cos_sin(block.T)
        cosine[at, :] = c
        sine[at, :] = s
        return carry

    lax.fori_loop(0, phases.shape[2] // 128, angles, 0)
    for level in range(levels):

        @pl.when(pair == level // 2)
        def _():
            pair_level(state, cosine, sine, weights[level % 2], 2**level, level % 2)


def core_kernel(parity_ref, own, partner, cosine, sine, weights, out):
    odd = parity_ref[0] == 1
    w = weights[0]

    def step(i, carry):
        at = pl.ds(pl.multiple_of(i * CHUNK, CHUNK), CHUNK)
        mine, other = own[at, :], partner[at, :]
        low = jnp.where(odd, other, mine)
        high = jnp.where(odd, mine, other)
        new = dot3(jnp.concatenate([low, high], axis=1), w)
        out[at, :] = rotate(new, cosine[at, :], sine[at, :], 1)
        return carry

    lax.fori_loop(0, own.shape[0] // CHUNK, step, 0)


def angles_kernel(angles, cosine, sine):
    c, s = cos_sin(angles[...].reshape(-1, 128))
    cosine[0] = c
    sine[0] = s


def final_kernel(levels, boxes, source, cosine, sine, weights, out, state):
    pair = pl.program_id(0)

    @pl.when(pair == 0)
    def _():
        state[...] = source[...]

    def put(i, low, high):
        n = CHUNK // boxes
        at = i * n
        half = out.shape[1] // 2
        out[:, pl.ds(pl.multiple_of(at, 8), n), :] = jnp.swapaxes(low.reshape(n, boxes, 128), 0, 1)
        out[:, pl.ds(pl.multiple_of(half + at, 8), n), :] = jnp.swapaxes(high.reshape(n, boxes, 128), 0, 1)

    for level in range(levels):

        @pl.when(pair == level // 2)
        def _():
            pair_level(
                state,
                cosine.at[0],
                sine.at[0],
                weights[level % 2],
                boxes * 2 ** (level + 1),
                level % 2,
                put if level == levels - 1 else None,
            )


def params():
    return pltpu.CompilerParams(vmem_limit_bytes=VMEM)


def cost(microseconds, moved):
    return pl.CostEstimate(flops=int(microseconds * 1e9), bytes_accessed=moved, transcendentals=0)


def per_device(source, interp_maps, phases):
    box_dev, columns = source.shape
    f32 = jnp.float32
    devices = lax.axis_size("narrow") * lax.axis_size("wide")
    per_peer = box_dev // devices
    local = box_dev.bit_length() - 1
    levels = interp_maps.shape[0]
    first = local + 1
    pairs = (levels - first) // 2
    turned = jnp.transpose(phases, (0, 2, 1))
    points = turned.shape[1]

    packed = pl.pallas_call(
        pack_kernel,
        grid=(pairs, 2),
        in_specs=[pl.BlockSpec((2, points, box_dev // 2), lambda k, h: (first // 2 + k, 0, h))],
        out_specs=pl.BlockSpec((devices // 2, per_peer, columns), lambda k, h: (h, k, 0)),
        out_shape=jax.ShapeDtypeStruct((devices, pairs * per_peer, columns), f32),
        compiler_params=params(),
        cost_estimate=cost(2, 6 << 20),
        name="pack_phases",
    )(turned)
    arrived = lax.all_to_all(packed, AXES, split_axis=0, concat_axis=0, tiled=True)

    weights = pl.pallas_call(
        weights_kernel,
        grid=(levels,),
        in_specs=[pl.BlockSpec((1, 2, 2, columns, columns), lambda l: (l, 0, 0, 0, 0))],
        out_specs=pl.BlockSpec((1, 4 * columns, 2 * columns), lambda l: (l, 0, 0)),
        out_shape=jax.ShapeDtypeStruct((levels, 4 * columns, 2 * columns), jnp.bfloat16),
        compiler_params=params(),
        cost_estimate=cost(4, 9 << 20),
        name="split_maps",
    )(interp_maps)

    whole = jax.ShapeDtypeStruct((box_dev, columns), f32)
    whole_spec = pl.BlockSpec((box_dev, columns), lambda k: (0, 0))
    state, cosine, sine = pl.pallas_call(
        functools.partial(local_kernel, local),
        grid=(first // 2,),
        in_specs=[
            whole_spec,
            pl.BlockSpec((2, points, box_dev), lambda k: (k, 0, 0)),
            pl.BlockSpec((2, 4 * columns, 2 * columns), lambda k: (k, 0, 0)),
        ],
        out_specs=[whole_spec] * 3,
        out_shape=[whole] * 3,
        compiler_params=params(),
        cost_estimate=cost(20, 18 << 20),
        name="local_levels",
    )(source, turned, weights)

    wide = lax.axis_size("wide")
    partner = lax.ppermute(state, "wide", [(i, i ^ 1) for i in range(wide)])
    parity = jnp.reshape(lax.axis_index("wide") & 1, (1,)).astype(jnp.int32)
    state = pl.pallas_call(
        core_kernel,
        grid_spec=pltpu.PrefetchScalarGridSpec(
            num_scalar_prefetch=1,
            grid=(1,),
            in_specs=[pl.BlockSpec((box_dev, columns), lambda k, p: (0, 0))] * 4
            + [pl.BlockSpec((1, 4 * columns, columns), lambda k, p: (first - 1, 0, p[0]))],
            out_specs=pl.BlockSpec((box_dev, columns), lambda k, p: (0, 0)),
        ),
        out_shape=whole,
        compiler_params=params(),
        cost_estimate=cost(3, 5 << 20),
        name="core_level",
    )(parity, state, partner, cosine, sine, weights)

    state, arrived = lax.optimization_barrier((state, arrived))
    state = lax.all_to_all(state.reshape(devices, per_peer, columns), AXES, split_axis=0, concat_axis=0, tiled=True)

    blocks = 4
    packed_rows = jax.ShapeDtypeStruct((pairs, box_dev, columns), f32)
    cosine, sine = pl.pallas_call(
        angles_kernel,
        grid=(pairs, blocks),
        in_specs=[pl.BlockSpec((devices // blocks, per_peer, columns), lambda k, b: (b, k, 0))],
        out_specs=[pl.BlockSpec((1, box_dev // blocks, columns), lambda k, b: (k, b, 0))] * 2,
        out_shape=[packed_rows] * 2,
        compiler_params=params(),
        cost_estimate=cost(6, 9 << 20),
        name="angles",
    )(arrived)

    out = pl.pallas_call(
        functools.partial(final_kernel, levels - first, per_peer),
        grid=(pairs,),
        in_specs=[
            whole_spec,
            pl.BlockSpec((1, box_dev, columns), lambda k: (k, 0, 0)),
            pl.BlockSpec((1, box_dev, columns), lambda k: (k, 0, 0)),
            pl.BlockSpec((2, 4 * columns, 2 * columns), lambda k: (first // 2 + k, 0, 0)),
        ],
        out_specs=pl.BlockSpec((per_peer, devices, columns), lambda k: (0, 0, 0)),
        out_shape=jax.ShapeDtypeStruct((per_peer, devices, columns), f32),
        scratch_shapes=[pltpu.VMEM((box_dev, columns), f32)],
        compiler_params=params(),
        cost_estimate=cost(6, 10 << 20),
        name="final_levels",
    )(state.reshape(box_dev, columns), cosine, sine, weights)
    return out.reshape(box_dev, columns)


def solution(mesh):
    in_specs = (P(AXES, None), P(), P(None, AXES, None))
    return jax.shard_map(per_device, mesh=mesh, in_specs=in_specs, out_specs=P(AXES, None), check_vma=False)
```

```python
import functools

import jax
import jax.numpy as jnp
from jax import lax
from jax.experimental import pallas as pl
from jax.experimental.pallas import tpu as pltpu
from jax.sharding import PartitionSpec as P

AXES = ("narrow", "wide")
SIN_HALF = (0.9999999957157406, -0.041666644924359314, 0.0005208156633383668, -3.095163447075199e-06, 1.0176428087056766e-08)
COS_HALF = (0.9999999532465265, -0.12499976265264102, 0.002603973680502671, -2.1646354078657635e-05, 9.044205735375736e-08)
CHUNK = 256
VMEM = 40 * 2**20


def horner(coefficients, z):
    total = jnp.full_like(z, coefficients[-1])
    for c in coefficients[-2::-1]:
        total = total * z + c
    return total


def cos_sin(x):
    z = x * x
    s = x * horner(SIN_HALF, z)
    c = horner(COS_HALF, z)
    return 1.0 - 0.5 * (s * s), s * c


def spread(cosine, sine, parity):
    left = lax.broadcasted_iota(jnp.int32, cosine.shape, 1) < 64
    c_roll = pltpu.roll(cosine, 64, 1)
    s_roll = pltpu.roll(sine, 64, 1)
    if parity == 0:
        return jnp.where(left, cosine, c_roll), jnp.where(left, -sine, s_roll)
    return jnp.where(left, c_roll, cosine), jnp.where(left, -s_roll, sine)


def rotate(values, cosine, sine, parity):
    c2, s2 = spread(cosine, sine, parity)
    return values * c2 + pltpu.roll(values, 64, 1) * s2


def dot3(x, w):
    k = x.shape[1]
    upper = x.astype(jnp.bfloat16)
    lower = (x - upper.astype(jnp.float32)).astype(jnp.bfloat16)
    w_up, w_low = w[:k], w[k:]
    dot = functools.partial(jnp.dot, preferred_element_type=jnp.float32)
    return dot(upper, w_up) + (dot(lower, w_up) + dot(upper, w_low))


def row_slices(stride, step, n=CHUNK):
    if stride >= n:
        per = stride // n
        return [pl.ds((step // per) * 2 * stride + (step % per) * n, n)]
    base = step * 2 * n
    if stride >= 8:
        return [pl.ds(base + j * 2 * stride, stride) for j in range(n // stride)]
    return [pl.ds(base + o, n // stride, stride=2 * stride) for o in range(stride)]


def shifted(s, by):
    return pl.ds(s.start + by, s.size, stride=s.stride)


def load_pairs(ref, slices, stride):
    def cat(parts):
        return parts[0] if len(parts) == 1 else jnp.concatenate(parts, axis=0)

    return cat([ref[s, :] for s in slices]), cat([ref[shifted(s, stride), :] for s in slices])


def store_pairs(ref, slices, stride, low, high):
    at = 0
    for s in slices:
        ref[s, :] = low[at : at + s.size]
        ref[shifted(s, stride), :] = high[at : at + s.size]
        at += s.size


def pair_level(state, cosine, sine, w, stride, parity, put=None, ready=None):
    rows = state.shape[0]

    for i in range(rows // (2 * CHUNK)):
        if ready is not None:
            ready(i)
        slices = row_slices(stride, i)
        low, high = load_pairs(state, slices, stride)
        new = dot3(jnp.concatenate([low, high], axis=1), w)
        c_low, c_high = load_pairs(cosine, slices, stride)
        s_low, s_high = load_pairs(sine, slices, stride)
        low = rotate(new[:, :128], c_low, s_low, parity)
        high = rotate(new[:, 128:], c_high, s_high, parity)
        if put is None:
            store_pairs(state, slices, stride, low, high)
        else:
            put(i, low, high)


def pack_kernel(first, parts, phases, out, angles, packed, come, gone):
    levels, _, columns = angles.shape
    size = columns // parts
    devices = size // 16

    def arrive(i):
        at = pl.ds(i * size, size)
        return pltpu.make_async_copy(phases.at[pl.ds(first, levels), :, at], angles.at[:, :, at], come.at[i])

    def leave(i):
        at = pl.ds(i * devices, devices)
        return pltpu.make_async_copy(packed.at[at], out.at[at], gone.at[i])

    for i in range(parts):
        arrive(i).start()
    for i in range(parts):
        arrive(i).wait()
        for j in range(i * size // 128, (i + 1) * size // 128):
            for k in range(levels // 2):
                at = pl.ds(j * 128, 128)
                block = jnp.concatenate([angles[2 * k, :, at], angles[2 * k + 1, :, at]], axis=0)
                packed[pl.ds(j * 8, 8), pl.ds(k * 16, 16), :] = block.T.reshape(8, 16, 128)
        leave(i).start()
    for i in range(parts):
        leave(i).wait()


def split_map(maps):
    w = jnp.concatenate([jnp.concatenate([maps[0, i], maps[1, i]], axis=1) for i in range(2)], axis=0)
    upper = w.astype(jnp.bfloat16)
    return jnp.concatenate([upper, (w - upper.astype(jnp.float32)).astype(jnp.bfloat16)], axis=0)


def local_kernel(levels, source, phases, maps, state, cosine, sine):
    pair = pl.program_id(0)

    @pl.when(pair == 0)
    def _():
        state[...] = source[...]

    def angles(j, carry):
        at = pl.ds(pl.multiple_of(j * 128, 128), 128)
        block = jnp.concatenate([phases[0, :, at], phases[1, :, at]], axis=0)
        c, s = cos_sin(block.T)
        cosine[at, :] = c
        sine[at, :] = s
        return carry

    lax.fori_loop(0, phases.shape[2] // 128, angles, 0, unroll=4)
    for level in range(levels):

        @pl.when(pair == level // 2)
        def _():
            pair_level(state, cosine, sine, split_map(maps[level % 2]), 2**level, level % 2)


def core_kernel(parity_ref, own, partner, cosine, sine, maps, out):
    odd = parity_ref[0] == 1
    w = jnp.concatenate([maps[0, 0, 0], maps[0, 0, 1]], axis=0)
    upper = w.astype(jnp.bfloat16)
    w = jnp.concatenate([upper, (w - upper.astype(jnp.float32)).astype(jnp.bfloat16)], axis=0)

    def step(i, carry):
        at = pl.ds(pl.multiple_of(i * CHUNK, CHUNK), CHUNK)
        mine, other = own[at, :], partner[at, :]
        low = jnp.where(odd, other, mine)
        high = jnp.where(odd, mine, other)
        new = dot3(jnp.concatenate([low, high], axis=1), w)
        out[at, :] = rotate(new, cosine[at, :], sine[at, :], 1)
        return carry

    lax.fori_loop(0, own.shape[0] // CHUNK, step, 0)


def angles_kernel(angles, maps, cosine, sine, weights):
    block = pl.program_id(0)

    @pl.when(block == 0)
    def _():
        for level in range(weights.shape[0]):
            weights[level] = split_map(maps[level])

    rows = angles.shape[0] * 16
    for k in range(cosine.shape[0]):
        at = pl.ds(pl.multiple_of(block * rows, rows), rows)
        c, s = cos_sin(angles[:, pl.ds(k * 16, 16), :].reshape(rows, 128))
        cosine[k, at, :] = c
        sine[k, at, :] = s


def final_kernel(levels, boxes, source, cosine, sine, weights, out, state, turned, come, gone):
    rows = state.shape[0]
    steps = rows // (2 * CHUNK)
    n = CHUNK // boxes
    half = out.shape[1] // 2

    def arrive(i):
        at = pl.ds(i * 2 * CHUNK, 2 * CHUNK)
        return pltpu.make_async_copy(source.at[at], state.at[at], come.at[i])

    def leave(i, upper):
        at = pl.ds(upper * half + i * n, n)
        return pltpu.make_async_copy(turned.at[:, at, :], out.at[:, at, :], gone.at[2 * i + upper])

    def put(i, low, high):
        for upper, values in enumerate((low, high)):
            turned[:, pl.ds(upper * half + i * n, n), :] = jnp.swapaxes(values.reshape(n, boxes, 128), 0, 1)
            leave(i, upper).start()

    for i in range(steps):
        arrive(i).start()
    for level in range(levels):
        pair_level(
            state,
            cosine.at[level // 2],
            sine.at[level // 2],
            weights[level],
            boxes * 2 ** (level + 1),
            level % 2,
            put if level == levels - 1 else None,
            (lambda i: arrive(i).wait()) if level == 0 else None,
        )
    for i in range(steps):
        leave(i, 0).wait()
        leave(i, 1).wait()


def params():
    return pltpu.CompilerParams(vmem_limit_bytes=VMEM)


def cost(microseconds, moved):
    return pl.CostEstimate(flops=int(microseconds * 1e9), bytes_accessed=moved, transcendentals=0)


def per_device(source, interp_maps, phases):
    box_dev, columns = source.shape
    f32 = jnp.float32
    devices = lax.axis_size("narrow") * lax.axis_size("wide")
    per_peer = box_dev // devices
    local = box_dev.bit_length() - 1
    levels = interp_maps.shape[0]
    first = local + 1
    pairs = (levels - first) // 2
    turned = jnp.transpose(phases, (0, 2, 1))
    points = turned.shape[1]

    parts = 4
    packed = pl.pallas_call(
        functools.partial(pack_kernel, first, parts),
        in_specs=[pl.BlockSpec(memory_space=pl.ANY)],
        out_specs=pl.BlockSpec(memory_space=pl.ANY),
        out_shape=jax.ShapeDtypeStruct((devices, pairs * per_peer, columns), f32),
        scratch_shapes=[
            pltpu.VMEM((2 * pairs, points, box_dev), f32),
            pltpu.VMEM((devices, pairs * per_peer, columns), f32),
            pltpu.SemaphoreType.DMA((parts,)),
            pltpu.SemaphoreType.DMA((parts,)),
        ],
        compiler_params=params(),
        cost_estimate=cost(2, 6 << 20),
        name="pack_phases",
    )(turned)
    arrived = lax.all_to_all(packed, AXES, split_axis=0, concat_axis=0, tiled=True)

    whole = jax.ShapeDtypeStruct((box_dev, columns), f32)
    whole_spec = pl.BlockSpec((box_dev, columns), lambda k: (0, 0))
    state, cosine, sine = pl.pallas_call(
        functools.partial(local_kernel, local),
        grid=(first // 2,),
        in_specs=[
            whole_spec,
            pl.BlockSpec((2, points, box_dev), lambda k: (k, 0, 0)),
            pl.BlockSpec((2, 2, 2, columns, columns), lambda k: (k, 0, 0, 0, 0)),
        ],
        out_specs=[whole_spec] * 3,
        out_shape=[whole] * 3,
        compiler_params=params(),
        cost_estimate=cost(20, 18 << 20),
        name="local_levels",
    )(source, turned, interp_maps)

    wide = lax.axis_size("wide")
    partner = lax.ppermute(state, "wide", [(i, i ^ 1) for i in range(wide)])
    parity = jnp.reshape(lax.axis_index("wide") & 1, (1,)).astype(jnp.int32)
    state = pl.pallas_call(
        core_kernel,
        grid_spec=pltpu.PrefetchScalarGridSpec(
            num_scalar_prefetch=1,
            grid=(4,),
            in_specs=[pl.BlockSpec((box_dev // 4, columns), lambda k, p: (k, 0))] * 4
            + [pl.BlockSpec((1, 1, 2, columns, columns), lambda k, p: (first - 1, p[0], 0, 0, 0))],
            out_specs=pl.BlockSpec((box_dev // 4, columns), lambda k, p: (k, 0)),
        ),
        out_shape=whole,
        compiler_params=params(),
        cost_estimate=cost(3, 5 << 20),
        name="core_level",
    )(parity, state, partner, cosine, sine, interp_maps)

    state, arrived = lax.optimization_barrier((state, arrived))
    state = lax.all_to_all(state.reshape(devices, per_peer, columns), AXES, split_axis=0, concat_axis=0, tiled=True)

    blocks = 4
    packed_rows = pltpu.VMEM((pairs, box_dev, columns), f32)
    in_vmem = pl.BlockSpec(memory_space=pltpu.VMEM)
    cosine, sine, weights = pl.pallas_call(
        angles_kernel,
        grid=(blocks,),
        in_specs=[
            pl.BlockSpec((devices // blocks, pairs * per_peer, columns), lambda b: (b, 0, 0)),
            pl.BlockSpec((2 * pairs, 2, 2, columns, columns), lambda b: (first // (2 * pairs), 0, 0, 0, 0)),
        ],
        out_specs=[in_vmem] * 3,
        out_shape=[packed_rows] * 2 + [pltpu.VMEM((2 * pairs, 4 * columns, 2 * columns), jnp.bfloat16)],
        compiler_params=params(),
        cost_estimate=cost(6, 9 << 20),
        name="angles",
    )(arrived, interp_maps)

    steps = box_dev // (2 * CHUNK)
    out = pl.pallas_call(
        functools.partial(final_kernel, levels - first, per_peer),
        in_specs=[pl.BlockSpec(memory_space=pl.ANY)] + [in_vmem] * 3,
        out_specs=pl.BlockSpec(memory_space=pl.ANY),
        out_shape=jax.ShapeDtypeStruct((per_peer, devices, columns), f32),
        scratch_shapes=[
            pltpu.VMEM((box_dev, columns), f32),
            pltpu.VMEM((per_peer, devices, columns), f32),
            pltpu.SemaphoreType.DMA((steps,)),
            pltpu.SemaphoreType.DMA((2 * steps,)),
        ],
        compiler_params=params(),
        cost_estimate=cost(6, 10 << 20),
        name="final_levels",
    )(state.reshape(box_dev, columns), cosine, sine, weights)
    return out.reshape(box_dev, columns)


def solution(mesh):
    in_specs = (P(AXES, None), P(), P(None, AXES, None))
    return jax.shard_map(per_device, mesh=mesh, in_specs=in_specs, out_specs=P(AXES, None), check_vma=False)
```

```python
import functools

import jax
import jax.numpy as jnp
from jax import lax
from jax.experimental import pallas as pl
from jax.experimental.pallas import tpu as pltpu
from jax.sharding import PartitionSpec as P

AXES = ("narrow", "wide")
SIN_HALF = (0.9999999957157406, -0.041666644924359314, 0.0005208156633383668, -3.095163447075199e-06, 1.0176428087056766e-08)
COS_HALF = (0.9999999532465265, -0.12499976265264102, 0.002603973680502671, -2.1646354078657635e-05, 9.044205735375736e-08)
CHUNK = 256
VMEM = 58 * 2**20


def horner(coefficients, z):
    total = jnp.full_like(z, coefficients[-1])
    for c in coefficients[-2::-1]:
        total = total * z + c
    return total


def cos_sin(x):
    z = x * x
    s = x * horner(SIN_HALF, z)
    c = horner(COS_HALF, z)
    return 1.0 - 0.5 * (s * s), s * c


def spread(cosine, sine, parity):
    left = lax.broadcasted_iota(jnp.int32, cosine.shape, 1) < 64
    c_roll = pltpu.roll(cosine, 64, 1)
    s_roll = pltpu.roll(sine, 64, 1)
    if parity == 0:
        return jnp.where(left, cosine, c_roll), jnp.where(left, -sine, s_roll)
    return jnp.where(left, c_roll, cosine), jnp.where(left, -s_roll, sine)


def rotate(values, cosine, sine, parity):
    c2, s2 = spread(cosine, sine, parity)
    return values * c2 + pltpu.roll(values, 64, 1) * s2


def dot3(x, w):
    upper = x.astype(jnp.bfloat16)
    lower = (x - upper.astype(jnp.float32)).astype(jnp.bfloat16)
    return jnp.dot(jnp.concatenate([upper, lower, upper], axis=1), w, preferred_element_type=jnp.float32)


def row_slices(stride, step, n=CHUNK):
    if stride >= n:
        per = stride // n
        return [pl.ds((step // per) * 2 * stride + (step % per) * n, n)]
    base = step * 2 * n
    if stride >= 8:
        return [pl.ds(base + j * 2 * stride, stride) for j in range(n // stride)]
    return [pl.ds(base + o, n // stride, stride=2 * stride) for o in range(stride)]


def shifted(s, by):
    return pl.ds(s.start + by, s.size, stride=s.stride)


def load_pairs(ref, slices, stride):
    def cat(parts):
        return parts[0] if len(parts) == 1 else jnp.concatenate(parts, axis=0)

    return cat([ref[s, :] for s in slices]), cat([ref[shifted(s, stride), :] for s in slices])


def store_pairs(ref, slices, stride, low, high):
    at = 0
    for s in slices:
        ref[s, :] = low[at : at + s.size]
        ref[shifted(s, stride), :] = high[at : at + s.size]
        at += s.size


def pair_level(state, cosine, sine, w, stride, parity, put=None, ready=None):
    rows = state.shape[0]

    for i in range(rows // (2 * CHUNK)):
        if ready is not None:
            ready(i)
        slices = row_slices(stride, i)
        low, high = load_pairs(state, slices, stride)
        new = dot3(jnp.concatenate([low, high], axis=1), w)
        c_low, c_high = load_pairs(cosine, slices, stride)
        s_low, s_high = load_pairs(sine, slices, stride)
        low = rotate(new[:, :128], c_low, s_low, parity)
        high = rotate(new[:, 128:], c_high, s_high, parity)
        if put is None:
            store_pairs(state, slices, stride, low, high)
        else:
            put(i, low, high)


def pack_kernel(first, parts, phases, out, angles, packed, come, gone):
    levels, _, columns = angles.shape
    size = columns // parts
    devices = size // 16

    def arrive(i):
        at = pl.ds(i * size, size)
        return pltpu.make_async_copy(phases.at[pl.ds(first, levels), :, at], angles.at[:, :, at], come.at[i])

    def leave(i):
        at = pl.ds(i * devices, devices)
        return pltpu.make_async_copy(packed.at[at], out.at[at], gone.at[i])

    for i in range(parts):
        arrive(i).start()
    for i in range(parts):
        arrive(i).wait()
        for j in range(i * size // 128, (i + 1) * size // 128):
            for k in range(levels // 2):
                at = pl.ds(j * 128, 128)
                block = jnp.concatenate([angles[2 * k, :, at], angles[2 * k + 1, :, at]], axis=0)
                packed[pl.ds(j * 8, 8), pl.ds(k * 16, 16), :] = block.T.reshape(8, 16, 128)
        leave(i).start()
    for i in range(parts):
        leave(i).wait()


def halves(w):
    upper = w.astype(jnp.bfloat16)
    return jnp.concatenate([upper, upper, (w - upper.astype(jnp.float32)).astype(jnp.bfloat16)], axis=0)


def split_map(maps):
    return halves(jnp.concatenate([jnp.concatenate([maps[0, i], maps[1, i]], axis=1) for i in range(2)], axis=0))


def split_map_planes(maps):
    real, imag = slice(0, 64), slice(64, 128)
    return halves(
        jnp.concatenate(
            [jnp.concatenate([maps[o, i][:, part] for part in (real, imag) for o in range(2)], axis=1) for i in range(2)], axis=0
        )
    )


def local_kernel(levels, source, phases, maps, state, cosine, sine):
    pair = pl.program_id(0)

    @pl.when(pair == 0)
    def _():
        state[...] = source[...]

    def angles(j, carry):
        at = pl.ds(pl.multiple_of(j * 128, 128), 128)
        block = jnp.concatenate([phases[0, :, at], phases[1, :, at]], axis=0)
        c, s = cos_sin(block.T)
        cosine[at, :] = c
        sine[at, :] = s
        return carry

    lax.fori_loop(0, phases.shape[2] // 128, angles, 0, unroll=4)
    for level in range(levels):

        @pl.when(pair == level // 2)
        def _():
            pair_level(state, cosine, sine, split_map(maps[level % 2]), 2**level, level % 2)


def core_kernel(parity_ref, own, partner, cosine, sine, maps, out):
    odd = parity_ref[0] == 1
    w = halves(jnp.concatenate([maps[0, 0, 0], maps[0, 0, 1]], axis=0))

    def step(i, carry):
        at = pl.ds(pl.multiple_of(i * CHUNK, CHUNK), CHUNK)
        mine, other = own[at, :], partner[at, :]
        low = jnp.where(odd, other, mine)
        high = jnp.where(odd, mine, other)
        new = dot3(jnp.concatenate([low, high], axis=1), w)
        out[at, :] = rotate(new, cosine[at, :], sine[at, :], 1)
        return carry

    lax.fori_loop(0, own.shape[0] // CHUNK, step, 0)


def angles_kernel(boxes, angles, maps, waves, weights, cos_rows, sin_rows):
    rows = cos_rows.shape[0]
    level = 2 * pl.program_id(0)
    c, s = cos_sin(angles[...].reshape(rows, 128))
    cos_rows[...] = c
    sin_rows[...] = s
    left = lax.broadcasted_iota(jnp.int32, (CHUNK, 128), 1) < 64
    for pair in range(3):

        @pl.when(pl.program_id(0) == pair)
        def _():
            for parity in range(2):
                stride = boxes * 2 ** (2 * pair + parity + 1)
                for i in range(rows // (2 * CHUNK)):
                    for which, here in enumerate((cos_rows, sin_rows)):
                        low, high = load_pairs(here, row_slices(stride, i), stride)
                        if parity == 0:
                            both = jnp.where(left, low, pltpu.roll(high, 64, 1))
                        else:
                            both = jnp.where(left, pltpu.roll(low, 64, 1), high)
                        waves[parity, which, pl.ds(i * CHUNK, CHUNK), :] = both

    for parity in range(2):
        weights[parity] = split_map_planes(maps[parity])


def plane_level(state, waves, w, stride, put=None):
    left = lax.broadcasted_iota(jnp.int32, (CHUNK, 128), 1) < 64
    for i in range(state.shape[0] // (2 * CHUNK)):
        slices = row_slices(stride, i)
        low, high = load_pairs(state, slices, stride)
        new = dot3(jnp.concatenate([low, high], axis=1), w)
        at = pl.ds(i * CHUNK, CHUNK)
        c, s = waves[0, at, :], waves[1, at, :]
        real, imag = new[:, :128], new[:, 128:]
        real, imag = real * c - imag * s, real * s + imag * c
        low = jnp.where(left, real, pltpu.roll(imag, 64, 1))
        high = jnp.where(left, pltpu.roll(real, 64, 1), imag)
        if put is None:
            store_pairs(state, slices, stride, low, high)
        else:
            put(i, low, high)


def final_kernel(levels, boxes, source, waves, weights, out, state, waves_here, w_here, turned, come, gone):
    steps = state.shape[0] // (2 * CHUNK)
    n = CHUNK // boxes
    half = out.shape[1] // 2

    def arrive(level):
        here = [
            pltpu.make_async_copy(weights.at[level], w_here.at[level], come.at[3 * level]),
            pltpu.make_async_copy(waves.at[level], waves_here.at[level], come.at[3 * level + 1]),
        ]
        return here + ([pltpu.make_async_copy(source, state, come.at[2])] if level == 0 else [])

    def leave(i, upper):
        at = pl.ds(upper * half + i * n, n)
        return pltpu.make_async_copy(turned.at[:, at, :], out.at[:, at, :], gone.at[2 * i + upper])

    def put(i, low, high):
        for upper, values in enumerate((low, high)):
            turned[:, pl.ds(upper * half + i * n, n), :] = jnp.swapaxes(values.reshape(n, boxes, 128), 0, 1)
            leave(i, upper).start()

    for level in range(levels):
        for copy in arrive(level):
            copy.start()
    for level in range(levels):
        for copy in arrive(level):
            copy.wait()
        plane_level(state, waves_here.at[level], w_here[level], boxes * 2 ** (level + 1), put if level == levels - 1 else None)
    for i in range(steps):
        leave(i, 0).wait()
        leave(i, 1).wait()


def params():
    return pltpu.CompilerParams(vmem_limit_bytes=VMEM)


def cost(microseconds, moved):
    return pl.CostEstimate(flops=int(microseconds * 1e9), bytes_accessed=moved, transcendentals=0)


def per_device(source, interp_maps, phases):
    box_dev, columns = source.shape
    f32 = jnp.float32
    devices = lax.axis_size("narrow") * lax.axis_size("wide")
    per_peer = box_dev // devices
    local = box_dev.bit_length() - 1
    levels = interp_maps.shape[0]
    first = local + 1
    pairs = (levels - first) // 2
    turned = jnp.transpose(phases, (0, 2, 1))
    points = turned.shape[1]

    parts = 4
    packed = pl.pallas_call(
        functools.partial(pack_kernel, first, parts),
        in_specs=[pl.BlockSpec(memory_space=pl.ANY)],
        out_specs=pl.BlockSpec(memory_space=pl.ANY),
        out_shape=jax.ShapeDtypeStruct((devices, pairs * per_peer, columns), f32),
        scratch_shapes=[
            pltpu.VMEM((2 * pairs, points, box_dev), f32),
            pltpu.VMEM((devices, pairs * per_peer, columns), f32),
            pltpu.SemaphoreType.DMA((parts,)),
            pltpu.SemaphoreType.DMA((parts,)),
        ],
        compiler_params=params(),
        cost_estimate=cost(2, 6 << 20),
        name="pack_phases",
    )(turned)
    arrived = lax.all_to_all(packed, AXES, split_axis=0, concat_axis=0, tiled=True)

    whole = jax.ShapeDtypeStruct((box_dev, columns), f32)
    whole_spec = pl.BlockSpec((box_dev, columns), lambda k: (0, 0))
    state, cosine, sine = pl.pallas_call(
        functools.partial(local_kernel, local),
        grid=(first // 2,),
        in_specs=[
            whole_spec,
            pl.BlockSpec((2, points, box_dev), lambda k: (k, 0, 0)),
            pl.BlockSpec((2, 2, 2, columns, columns), lambda k: (k, 0, 0, 0, 0)),
        ],
        out_specs=[whole_spec] * 3,
        out_shape=[whole] * 3,
        compiler_params=params(),
        cost_estimate=cost(20, 18 << 20),
        name="local_levels",
    )(source, turned, interp_maps)

    wide = lax.axis_size("wide")
    partner = lax.ppermute(state, "wide", [(i, i ^ 1) for i in range(wide)])
    parity = jnp.reshape(lax.axis_index("wide") & 1, (1,)).astype(jnp.int32)
    state = pl.pallas_call(
        core_kernel,
        grid_spec=pltpu.PrefetchScalarGridSpec(
            num_scalar_prefetch=1,
            grid=(4,),
            in_specs=[pl.BlockSpec((box_dev // 4, columns), lambda k, p: (k, 0))] * 4
            + [pl.BlockSpec((1, 1, 2, columns, columns), lambda k, p: (first - 1, p[0], 0, 0, 0))],
            out_specs=pl.BlockSpec((box_dev // 4, columns), lambda k, p: (k, 0)),
        ),
        out_shape=whole,
        compiler_params=params(),
        cost_estimate=cost(3, 5 << 20),
        name="core_level",
    )(parity, state, partner, cosine, sine, interp_maps)

    state, arrived = lax.optimization_barrier((state, arrived))
    state = lax.all_to_all(state.reshape(devices, per_peer, columns), AXES, split_axis=0, concat_axis=0, tiled=True)

    waves_shape = (2 * pairs, 2, box_dev // 2, columns)
    waves, weights = pl.pallas_call(
        functools.partial(angles_kernel, per_peer),
        grid=(pairs,),
        in_specs=[
            pl.BlockSpec((devices, per_peer, columns), lambda k: (0, k, 0)),
            pl.BlockSpec((2, 2, 2, columns, columns), lambda k: (first // 2 + k, 0, 0, 0, 0)),
        ],
        out_specs=[
            pl.BlockSpec((2, *waves_shape[1:]), lambda k: (k, 0, 0, 0)),
            pl.BlockSpec((2, 6 * columns, 2 * columns), lambda k: (k, 0, 0)),
        ],
        out_shape=[jax.ShapeDtypeStruct(waves_shape, f32), jax.ShapeDtypeStruct((2 * pairs, 6 * columns, 2 * columns), jnp.bfloat16)],
        scratch_shapes=[pltpu.VMEM((box_dev, columns), f32)] * 2,
        compiler_params=params(),
        cost_estimate=cost(6, 9 << 20),
        name="angles",
    )(arrived, interp_maps)

    steps = box_dev // (2 * CHUNK)
    out = pl.pallas_call(
        functools.partial(final_kernel, levels - first, per_peer),
        in_specs=[pl.BlockSpec(memory_space=pl.ANY)] * 3,
        out_specs=pl.BlockSpec(memory_space=pl.ANY),
        out_shape=jax.ShapeDtypeStruct((per_peer, devices, columns), f32),
        scratch_shapes=[
            pltpu.VMEM((box_dev, columns), f32),
            pltpu.VMEM(waves_shape, f32),
            pltpu.VMEM((2 * pairs, 6 * columns, 2 * columns), jnp.bfloat16),
            pltpu.VMEM((per_peer, devices, columns), f32),
            pltpu.SemaphoreType.DMA((6 * pairs,)),
            pltpu.SemaphoreType.DMA((2 * steps,)),
        ],
        compiler_params=params(),
        cost_estimate=cost(6, 10 << 20),
        name="final_levels",
    )(state.reshape(box_dev, columns), waves, weights)
    return out.reshape(box_dev, columns)


def solution(mesh):
    in_specs = (P(AXES, None), P(), P(None, AXES, None))
    return jax.shard_map(per_device, mesh=mesh, in_specs=in_specs, out_specs=P(AXES, None), check_vma=False)
```

```python
import functools

import jax
import jax.numpy as jnp
from jax import lax
from jax.experimental import pallas as pl
from jax.experimental.pallas import tpu as pltpu
from jax.sharding import PartitionSpec as P

AXES = ("narrow", "wide")
SIN_HALF = (0.9999999957157406, -0.041666644924359314, 0.0005208156633383668, -3.095163447075199e-06, 1.0176428087056766e-08)
COS_HALF = (0.9999999532465265, -0.12499976265264102, 0.002603973680502671, -2.1646354078657635e-05, 9.044205735375736e-08)
CHUNK = 256
VMEM = 58 * 2**20


def horner(coefficients, z):
    total = jnp.full_like(z, coefficients[-1])
    for c in coefficients[-2::-1]:
        total = total * z + c
    return total


def cos_sin(x):
    z = x * x
    s = x * horner(SIN_HALF, z)
    c = horner(COS_HALF, z)
    return 1.0 - 0.5 * (s * s), s * c


def spread(cosine, sine, parity):
    left = lax.broadcasted_iota(jnp.int32, cosine.shape, 1) < 64
    c_roll = pltpu.roll(cosine, 64, 1)
    s_roll = pltpu.roll(sine, 64, 1)
    if parity == 0:
        return jnp.where(left, cosine, c_roll), jnp.where(left, -sine, s_roll)
    return jnp.where(left, c_roll, cosine), jnp.where(left, -s_roll, sine)


def rotate(values, cosine, sine, parity):
    c2, s2 = spread(cosine, sine, parity)
    return values * c2 + pltpu.roll(values, 64, 1) * s2


def dot3(x, w):
    upper = x.astype(jnp.bfloat16)
    lower = (x - upper.astype(jnp.float32)).astype(jnp.bfloat16)
    w = jnp.concatenate([w[: x.shape[1]], w], axis=0)
    return jnp.dot(jnp.concatenate([upper, lower, upper], axis=1), w, preferred_element_type=jnp.float32)


def row_slices(stride, step, n=CHUNK):
    if stride >= n:
        per = stride // n
        return [pl.ds((step // per) * 2 * stride + (step % per) * n, n)]
    base = step * 2 * n
    if stride >= 8:
        return [pl.ds(base + j * 2 * stride, stride) for j in range(n // stride)]
    return [pl.ds(base + o, n // stride, stride=2 * stride) for o in range(stride)]


def shifted(s, by):
    return pl.ds(s.start + by, s.size, stride=s.stride)


def load_pairs(ref, slices, stride):
    def cat(parts):
        return parts[0] if len(parts) == 1 else jnp.concatenate(parts, axis=0)

    return cat([ref[s, :] for s in slices]), cat([ref[shifted(s, stride), :] for s in slices])


def store_pairs(ref, slices, stride, low, high):
    at = 0
    for s in slices:
        ref[s, :] = low[at : at + s.size]
        ref[shifted(s, stride), :] = high[at : at + s.size]
        at += s.size


def pair_level(state, cosine, sine, w, stride, parity, put=None, ready=None):
    rows = state.shape[0]

    for i in range(rows // (2 * CHUNK)):
        if ready is not None:
            ready(i)
        slices = row_slices(stride, i)
        low, high = load_pairs(state, slices, stride)
        new = dot3(jnp.concatenate([low, high], axis=1), w)
        c_low, c_high = load_pairs(cosine, slices, stride)
        s_low, s_high = load_pairs(sine, slices, stride)
        low = rotate(new[:, :128], c_low, s_low, parity)
        high = rotate(new[:, 128:], c_high, s_high, parity)
        if put is None:
            store_pairs(state, slices, stride, low, high)
        else:
            put(i, low, high)


def pack_kernel(first, parts, phases, out, angles, packed, come, gone):
    levels, _, columns = angles.shape
    size = columns // parts
    devices = size // 16

    def arrive(i):
        at = pl.ds(i * size, size)
        return pltpu.make_async_copy(phases.at[pl.ds(first, levels), :, at], angles.at[:, :, at], come.at[i])

    def leave(i):
        at = pl.ds(i * devices, devices)
        return pltpu.make_async_copy(packed.at[at], out.at[at], gone.at[i])

    for i in range(parts):
        arrive(i).start()
    for i in range(parts):
        arrive(i).wait()
        for j in range(i * size // 128, (i + 1) * size // 128):
            for k in range(levels // 2):
                at = pl.ds(j * 128, 128)
                block = jnp.concatenate([angles[2 * k, :, at], angles[2 * k + 1, :, at]], axis=0)
                packed[pl.ds(j * 8, 8), pl.ds(k * 16, 16), :] = block.T.reshape(8, 16, 128)
        leave(i).start()
    for i in range(parts):
        leave(i).wait()


def halves(w):
    upper = w.astype(jnp.bfloat16)
    return jnp.concatenate([upper, (w - upper.astype(jnp.float32)).astype(jnp.bfloat16)], axis=0)


def split_map(maps):
    return halves(jnp.concatenate([jnp.concatenate([maps[0, i], maps[1, i]], axis=1) for i in range(2)], axis=0))


def split_map_planes(maps):
    real, imag = slice(0, 64), slice(64, 128)
    return halves(
        jnp.concatenate(
            [jnp.concatenate([maps[o, i][:, part] for part in (real, imag) for o in range(2)], axis=1) for i in range(2)], axis=0
        )
    )


def local_kernel(levels, source, phases, maps, state, cosine, sine):
    pair = pl.program_id(0)

    @pl.when(pair == 0)
    def _():
        state[...] = source[...]

    def angles(j, carry):
        at = pl.ds(pl.multiple_of(j * 128, 128), 128)
        block = jnp.concatenate([phases[0, :, at], phases[1, :, at]], axis=0)
        c, s = cos_sin(block.T)
        cosine[at, :] = c
        sine[at, :] = s
        return carry

    lax.fori_loop(0, phases.shape[2] // 128, angles, 0, unroll=4)
    for level in range(levels):

        @pl.when(pair == level // 2)
        def _():
            pair_level(state, cosine, sine, split_map(maps[level % 2]), 2**level, level % 2)


def core_kernel(parity_ref, own, partner, cosine, sine, maps, out):
    odd = parity_ref[0] == 1
    w = halves(jnp.concatenate([maps[0, 0, 0], maps[0, 0, 1]], axis=0))

    def step(i, carry):
        at = pl.ds(pl.multiple_of(i * CHUNK, CHUNK), CHUNK)
        mine, other = own[at, :], partner[at, :]
        low = jnp.where(odd, other, mine)
        high = jnp.where(odd, mine, other)
        new = dot3(jnp.concatenate([low, high], axis=1), w)
        out[at, :] = rotate(new, cosine[at, :], sine[at, :], 1)
        return carry

    lax.fori_loop(0, own.shape[0] // CHUNK, step, 0)


def angles_kernel(boxes, angles, maps, waves, weights, cos_rows, sin_rows):
    rows = cos_rows.shape[0]
    level = 2 * pl.program_id(0)
    c, s = cos_sin(angles[...].reshape(rows, 128))
    cos_rows[...] = c
    sin_rows[...] = s
    left = lax.broadcasted_iota(jnp.int32, (CHUNK, 128), 1) < 64
    for pair in range(3):

        @pl.when(pl.program_id(0) == pair)
        def _():
            for parity in range(2):
                stride = boxes * 2 ** (2 * pair + parity + 1)
                for i in range(rows // (2 * CHUNK)):
                    for which, here in enumerate((cos_rows, sin_rows)):
                        low, high = load_pairs(here, row_slices(stride, i), stride)
                        if parity == 0:
                            both = jnp.where(left, low, pltpu.roll(high, 64, 1))
                        else:
                            both = jnp.where(left, pltpu.roll(low, 64, 1), high)
                        waves[parity, which, pl.ds(i * CHUNK, CHUNK), :] = both

    for parity in range(2):
        weights[parity] = split_map_planes(maps[parity])


def plane_level(state, waves, w, stride, put=None):
    left = lax.broadcasted_iota(jnp.int32, (CHUNK, 128), 1) < 64
    for i in range(state.shape[0] // (2 * CHUNK)):
        slices = row_slices(stride, i)
        low, high = load_pairs(state, slices, stride)
        new = dot3(jnp.concatenate([low, high], axis=1), w)
        at = pl.ds(i * CHUNK, CHUNK)
        c, s = waves[0, at, :], waves[1, at, :]
        real, imag = new[:, :128], new[:, 128:]
        real, imag = real * c - imag * s, real * s + imag * c
        low = jnp.where(left, real, pltpu.roll(imag, 64, 1))
        high = jnp.where(left, pltpu.roll(real, 64, 1), imag)
        if put is None:
            store_pairs(state, slices, stride, low, high)
        else:
            put(i, low, high)


def final_kernel(levels, boxes, source, waves, weights, out, state, waves_here, w_here, turned, come, gone):
    steps = state.shape[0] // (2 * CHUNK)
    n = CHUNK // boxes
    half = out.shape[1] // 2

    def arrive(level):
        here = [
            pltpu.make_async_copy(weights.at[level], w_here.at[level], come.at[3 * level]),
            pltpu.make_async_copy(waves.at[level], waves_here.at[level], come.at[3 * level + 1]),
        ]
        return ([pltpu.make_async_copy(source, state, come.at[2])] if level == 0 else []) + here

    def leave(i, upper):
        at = pl.ds(upper * half + i * n, n)
        return pltpu.make_async_copy(turned.at[:, at, :], out.at[:, at, :], gone.at[2 * i + upper])

    def put(i, low, high):
        for upper, values in enumerate((low, high)):
            turned[:, pl.ds(upper * half + i * n, n), :] = jnp.swapaxes(values.reshape(n, boxes, 128), 0, 1)
            leave(i, upper).start()

    for level in range(levels):
        for copy in arrive(level):
            copy.start()
    groups = (0, 1, 3, 6)
    for level in range(levels):
        if level in groups:
            for other in range(level, groups[groups.index(level) + 1]):
                for copy in arrive(other):
                    copy.wait()
        plane_level(state, waves_here.at[level], w_here[level], boxes * 2 ** (level + 1), put if level == levels - 1 else None)
    for i in range(steps):
        leave(i, 0).wait()
        leave(i, 1).wait()


def params():
    return pltpu.CompilerParams(vmem_limit_bytes=VMEM)


def cost(microseconds, moved):
    return pl.CostEstimate(flops=int(microseconds * 1e9), bytes_accessed=moved, transcendentals=0)


def per_device(source, interp_maps, phases):
    box_dev, columns = source.shape
    f32 = jnp.float32
    devices = lax.axis_size("narrow") * lax.axis_size("wide")
    per_peer = box_dev // devices
    local = box_dev.bit_length() - 1
    levels = interp_maps.shape[0]
    first = local + 1
    pairs = (levels - first) // 2
    turned = jnp.transpose(phases, (0, 2, 1))
    points = turned.shape[1]

    parts = 4
    packed = pl.pallas_call(
        functools.partial(pack_kernel, first, parts),
        in_specs=[pl.BlockSpec(memory_space=pl.ANY)],
        out_specs=pl.BlockSpec(memory_space=pl.ANY),
        out_shape=jax.ShapeDtypeStruct((devices, pairs * per_peer, columns), f32),
        scratch_shapes=[
            pltpu.VMEM((2 * pairs, points, box_dev), f32),
            pltpu.VMEM((devices, pairs * per_peer, columns), f32),
            pltpu.SemaphoreType.DMA((parts,)),
            pltpu.SemaphoreType.DMA((parts,)),
        ],
        compiler_params=params(),
        cost_estimate=cost(2, 6 << 20),
        name="pack_phases",
    )(turned)
    arrived = lax.all_to_all(packed, AXES, split_axis=0, concat_axis=0, tiled=True)

    whole = jax.ShapeDtypeStruct((box_dev, columns), f32)
    whole_spec = pl.BlockSpec((box_dev, columns), lambda k: (0, 0))
    state, cosine, sine = pl.pallas_call(
        functools.partial(local_kernel, local),
        grid=(first // 2,),
        in_specs=[
            whole_spec,
            pl.BlockSpec((2, points, box_dev), lambda k: (k, 0, 0)),
            pl.BlockSpec((2, 2, 2, columns, columns), lambda k: (k, 0, 0, 0, 0)),
        ],
        out_specs=[whole_spec] * 3,
        out_shape=[whole] * 3,
        compiler_params=params(),
        cost_estimate=cost(20, 18 << 20),
        name="local_levels",
    )(source, turned, interp_maps)

    wide = lax.axis_size("wide")
    partner = lax.ppermute(state, "wide", [(i, i ^ 1) for i in range(wide)])
    parity = jnp.reshape(lax.axis_index("wide") & 1, (1,)).astype(jnp.int32)
    state = pl.pallas_call(
        core_kernel,
        grid_spec=pltpu.PrefetchScalarGridSpec(
            num_scalar_prefetch=1,
            grid=(4,),
            in_specs=[pl.BlockSpec((box_dev // 4, columns), lambda k, p: (k, 0))] * 4
            + [pl.BlockSpec((1, 1, 2, columns, columns), lambda k, p: (first - 1, p[0], 0, 0, 0))],
            out_specs=pl.BlockSpec((box_dev // 4, columns), lambda k, p: (k, 0)),
        ),
        out_shape=whole,
        compiler_params=params(),
        cost_estimate=cost(3, 5 << 20),
        name="core_level",
    )(parity, state, partner, cosine, sine, interp_maps)

    state, arrived = lax.optimization_barrier((state, arrived))
    state = lax.all_to_all(state.reshape(devices, per_peer, columns), AXES, split_axis=0, concat_axis=0, tiled=True)

    waves_shape = (2 * pairs, 2, box_dev // 2, columns)
    waves, weights = pl.pallas_call(
        functools.partial(angles_kernel, per_peer),
        grid=(pairs,),
        in_specs=[
            pl.BlockSpec((devices, per_peer, columns), lambda k: (0, k, 0)),
            pl.BlockSpec((2, 2, 2, columns, columns), lambda k: (first // 2 + k, 0, 0, 0, 0)),
        ],
        out_specs=[
            pl.BlockSpec((2, *waves_shape[1:]), lambda k: (k, 0, 0, 0)),
            pl.BlockSpec((2, 4 * columns, 2 * columns), lambda k: (k, 0, 0)),
        ],
        out_shape=[jax.ShapeDtypeStruct(waves_shape, f32), jax.ShapeDtypeStruct((2 * pairs, 4 * columns, 2 * columns), jnp.bfloat16)],
        scratch_shapes=[pltpu.VMEM((box_dev, columns), f32)] * 2,
        compiler_params=params(),
        cost_estimate=cost(6, 9 << 20),
        name="angles",
    )(arrived, interp_maps)

    steps = box_dev // (2 * CHUNK)
    out = pl.pallas_call(
        functools.partial(final_kernel, levels - first, per_peer),
        in_specs=[pl.BlockSpec(memory_space=pl.ANY)] * 3,
        out_specs=pl.BlockSpec(memory_space=pl.ANY),
        out_shape=jax.ShapeDtypeStruct((per_peer, devices, columns), f32),
        scratch_shapes=[
            pltpu.VMEM((box_dev, columns), f32),
            pltpu.VMEM(waves_shape, f32),
            pltpu.VMEM((2 * pairs, 4 * columns, 2 * columns), jnp.bfloat16),
            pltpu.VMEM((per_peer, devices, columns), f32),
            pltpu.SemaphoreType.DMA((6 * pairs,)),
            pltpu.SemaphoreType.DMA((2 * steps,)),
        ],
        compiler_params=params(),
        cost_estimate=cost(6, 10 << 20),
        name="final_levels",
    )(state.reshape(box_dev, columns), waves, weights)
    return out.reshape(box_dev, columns)


def solution(mesh):
    in_specs = (P(AXES, None), P(), P(None, AXES, None))
    return jax.shard_map(per_device, mesh=mesh, in_specs=in_specs, out_specs=P(AXES, None), check_vma=False)
```

```python
import functools

import jax
import jax.numpy as jnp
from jax import lax
from jax.experimental import pallas as pl
from jax.experimental.pallas import tpu as pltpu
from jax.sharding import PartitionSpec as P

AXES = ("narrow", "wide")
SIN_HALF = (0.9999999957157406, -0.041666644924359314, 0.0005208156633383668, -3.095163447075199e-06, 1.0176428087056766e-08)
COS_HALF = (0.9999999532465265, -0.12499976265264102, 0.002603973680502671, -2.1646354078657635e-05, 9.044205735375736e-08)
CHUNK = 256
VMEM = 58 * 2**20


def horner(coefficients, z):
    total = jnp.full_like(z, coefficients[-1])
    for c in coefficients[-2::-1]:
        total = total * z + c
    return total


def cos_sin(x):
    z = x * x
    s = x * horner(SIN_HALF, z)
    c = horner(COS_HALF, z)
    return 1.0 - 0.5 * (s * s), s * c


def dot3(x, w):
    upper = x.astype(jnp.bfloat16)
    lower = (x - upper.astype(jnp.float32)).astype(jnp.bfloat16)
    w = jnp.concatenate([w[: x.shape[1]], w], axis=0)
    return jnp.dot(jnp.concatenate([upper, lower, upper], axis=1), w, preferred_element_type=jnp.float32)


def row_slices(stride, step, n=CHUNK):
    if stride >= n:
        per = stride // n
        return [pl.ds((step // per) * 2 * stride + (step % per) * n, n)]
    base = step * 2 * n
    if stride >= 8:
        return [pl.ds(base + j * 2 * stride, stride) for j in range(n // stride)]
    return [pl.ds(base + o, n // stride, stride=2 * stride) for o in range(stride)]


def shifted(s, by):
    return pl.ds(s.start + by, s.size, stride=s.stride)


def load_pairs(ref, slices, stride):
    def cat(parts):
        return parts[0] if len(parts) == 1 else jnp.concatenate(parts, axis=0)

    return cat([ref[s, :] for s in slices]), cat([ref[shifted(s, stride), :] for s in slices])


def store_pairs(ref, slices, stride, low, high):
    at = 0
    for s in slices:
        ref[s, :] = low[at : at + s.size]
        ref[shifted(s, stride), :] = high[at : at + s.size]
        at += s.size


def pair_level(state, cosine, sine, w, stride, parity, put=None, ready=None):
    rows = state.shape[0]

    for i in range(rows // (2 * CHUNK)):
        if ready is not None:
            ready(i)
        slices = row_slices(stride, i)
        low, high = load_pairs(state, slices, stride)
        new = dot3(jnp.concatenate([low, high], axis=1), w)
        c_low, c_high = load_pairs(cosine, slices, stride)
        s_low, s_high = load_pairs(sine, slices, stride)
        low = rotate(new[:, :128], c_low, s_low, parity)
        high = rotate(new[:, 128:], c_high, s_high, parity)
        if put is None:
            store_pairs(state, slices, stride, low, high)
        else:
            put(i, low, high)


def pack_kernel(first, parts, phases, early, late, angles, packed, come, gone):
    levels, _, columns = angles.shape
    split = early.shape[1]
    rest = packed.shape[1] - split
    size = columns // parts
    devices = size // 16

    def arrive(i):
        at = pl.ds(i * size, size)
        return pltpu.make_async_copy(phases.at[pl.ds(first, levels), :, at], angles.at[:, :, at], come.at[i])

    def leave(i):
        at = pl.ds(i * devices, devices)
        return [
            pltpu.make_async_copy(packed.at[at, pl.ds(0, split), :], early.at[at], gone.at[2 * i]),
            pltpu.make_async_copy(packed.at[at, pl.ds(split, rest), :], late.at[at, pl.ds(rest, rest), :], gone.at[2 * i + 1]),
        ]

    for i in range(parts):
        arrive(i).start()
    for i in range(parts):
        arrive(i).wait()
        for j in range(i * size // 128, (i + 1) * size // 128):
            for k in range(levels // 2):
                at = pl.ds(j * 128, 128)
                block = jnp.concatenate([angles[2 * k, :, at], angles[2 * k + 1, :, at]], axis=0)
                packed[pl.ds(j * 8, 8), pl.ds(k * 16, 16), :] = block.T.reshape(8, 16, 128)
        for copy in leave(i):
            copy.start()
    for i in range(parts):
        for copy in leave(i):
            copy.wait()


def halves(w):
    upper = w.astype(jnp.bfloat16)
    return jnp.concatenate([upper, (w - upper.astype(jnp.float32)).astype(jnp.bfloat16)], axis=0)


def split_map_planes(maps):
    real, imag = slice(0, 64), slice(64, 128)
    return halves(
        jnp.concatenate(
            [jnp.concatenate([maps[o, i][:, part] for part in (real, imag) for o in range(2)], axis=1) for i in range(2)], axis=0
        )
    )


def join(low, high, parity):
    left = lax.broadcasted_iota(jnp.int32, low.shape, 1) < 64
    if parity == 0:
        return jnp.where(left, low, pltpu.roll(high, 64, 1))
    return jnp.where(left, pltpu.roll(low, 64, 1), high)


def mix(low, high, c, s, w):
    left = lax.broadcasted_iota(jnp.int32, low.shape, 1) < 64
    new = dot3(jnp.concatenate([low, high], axis=1), w)
    real, imag = new[:, :128], new[:, 128:]
    real, imag = real * c - imag * s, real * s + imag * c
    return jnp.where(left, real, pltpu.roll(imag, 64, 1)), jnp.where(left, pltpu.roll(real, 64, 1), imag)


def local_kernel(levels, source, phases, maps, state, last, cosine, sine):
    pair = pl.program_id(0)

    @pl.when(pair == 0)
    def _():
        state[...] = source[...]

    def angles(j, carry):
        at = pl.ds(pl.multiple_of(j * 128, 128), 128)
        block = jnp.concatenate([phases[0, :, at], phases[1, :, at]], axis=0)
        c, s = cos_sin(block.T)
        cosine[at, :] = c
        sine[at, :] = s
        return carry

    lax.fori_loop(0, phases.shape[2] // 128, angles, 0, unroll=True)
    for level in range(levels):

        @pl.when(pair == level // 2)
        def _():
            w = split_map_planes(maps[level % 2])
            stride = 2**level
            for i in range(state.shape[0] // (2 * CHUNK)):
                slices = row_slices(stride, i)
                low, high = load_pairs(state, slices, stride)
                c = join(*load_pairs(cosine, slices, stride), level % 2)
                s = join(*load_pairs(sine, slices, stride), level % 2)
                store_pairs(state, slices, stride, *mix(low, high, c, s, w))

    @pl.when(pair == levels // 2)
    def _():
        last[...] = join(cosine[...], sine[...], 1)


def core_kernel(parity_ref, own, partner, waves, maps, _, out):
    odd = parity_ref[0] == 1
    w = halves(jnp.concatenate([maps[0, 0, 0], maps[0, 0, 1]], axis=0))
    mine, other = own[...], partner[...]
    new = dot3(jnp.concatenate([jnp.where(odd, other, mine), jnp.where(odd, mine, other)], axis=1), w)
    left = lax.broadcasted_iota(jnp.int32, mine.shape, 1) < 64
    both = waves[...]
    turned = pltpu.roll(both, 64, 1)
    new = new * jnp.where(left, both, turned) + pltpu.roll(new, 64, 1) * jnp.where(left, -turned, both)
    out[...] = new.reshape(out.shape)


def join_rows(boxes, pair, parity, rows, put):
    stride = boxes * 2 ** (2 * pair + parity + 1)
    for i in range(rows.shape[0] // (2 * CHUNK)):
        put(pl.ds(i * CHUNK, CHUNK), join(*load_pairs(rows, row_slices(stride, i), stride), parity))


def angles_kernel(boxes, pairs, angles, waves, cos_rows, sin_rows):
    c, s = cos_sin(angles[...].reshape(cos_rows.shape))
    cos_rows[...] = c
    sin_rows[...] = s
    for pair in range(pairs):

        @pl.when(pl.program_id(0) == pair)
        def _():
            for parity in range(2):
                for which, rows in enumerate((cos_rows, sin_rows)):

                    def put(at, values, which=which, parity=parity):
                        waves[parity, which, at, :] = values

                    join_rows(boxes, pair, parity, rows, put)


def maps_kernel(maps, weights):
    for parity in range(2):
        weights[parity] = split_map_planes(maps[parity])


def final_kernel(
    levels, boxes, source, waves, weights, out, first, state, raw, cos_rows, sin_rows, waves_here, w_here, turned, come, gone
):
    rows = state.shape[0]
    steps = rows // (2 * CHUNK)
    n = CHUNK // boxes
    half = out.shape[1] // 2
    early = waves.shape[0]

    def arrive(level):
        here = [pltpu.make_async_copy(weights.at[level], w_here.at[level], come.at[2 * level])]
        if level < early:
            here.append(pltpu.make_async_copy(waves.at[level], waves_here.at[level], come.at[2 * level + 1]))
        return here

    def leave(i, upper):
        at = pl.ds(upper * half + i * n, n)
        return pltpu.make_async_copy(turned.at[:, at, :], out.at[:, at, :], gone.at[2 * i + upper])

    take = pltpu.make_async_copy(source.at[:, pl.ds(0, boxes), :], first, come.at[2 * levels])
    take_raw = pltpu.make_async_copy(source.at[:, pl.ds(boxes, boxes), :], raw, come.at[2 * levels + 1])
    take.start()
    for level in range(levels):
        for copy in arrive(level):
            copy.start()
        if level == 0:
            take_raw.start()
    groups = (0, 1, 3, levels)
    for level in range(levels):
        if level in groups:
            for other in range(level, groups[groups.index(level) + 1]):
                for copy in arrive(other):
                    copy.wait()
        if level == 0:
            take.wait()
        if level == 1:
            take_raw.wait()
            c, s = cos_sin(raw[...].reshape(rows, 128))
            cos_rows[...] = c
            sin_rows[...] = s
            for parity in range(2):
                for which, packed in enumerate((cos_rows, sin_rows)):

                    def put(at, values, which=which, parity=parity):
                        waves_here[early + parity, which, at, :] = values

                    join_rows(boxes, early // 2, parity, packed, put)
        stride = boxes * 2 ** (level + 1)
        for i in range(steps):
            slices = row_slices(stride, i)
            if level == 0:
                quads = first[pl.ds(2 * n * i, 2 * n)].reshape(n // 2, 2, stride, 128)
                low, high = quads[:, 0].reshape(CHUNK, 128), quads[:, 1].reshape(CHUNK, 128)
            else:
                low, high = load_pairs(state, slices, stride)
            at = pl.ds(i * CHUNK, CHUNK)
            low, high = mix(low, high, waves_here[level, 0, at, :], waves_here[level, 1, at, :], w_here[level])
            if level < levels - 1:
                store_pairs(state, slices, stride, low, high)
                continue
            for upper, values in enumerate((low, high)):
                turned[:, pl.ds(upper * half + i * n, n), :] = jnp.swapaxes(values.reshape(n, boxes, 128), 0, 1)
                leave(i, upper).start()
    for i in range(steps):
        leave(i, 0).wait()
        leave(i, 1).wait()


def params():
    return pltpu.CompilerParams(vmem_limit_bytes=VMEM)


def cost(microseconds, moved):
    return pl.CostEstimate(flops=int(microseconds * 1e9), bytes_accessed=moved, transcendentals=0)


def per_device(source, interp_maps, phases):
    box_dev, columns = source.shape
    f32 = jnp.float32
    devices = lax.axis_size("narrow") * lax.axis_size("wide")
    per_peer = box_dev // devices
    local = box_dev.bit_length() - 1
    levels = interp_maps.shape[0]
    first = local + 1
    pairs = (levels - first) // 2
    turned = jnp.transpose(phases, (0, 2, 1))
    points = turned.shape[1]

    early = (pairs - 1) * per_peer

    parts = 4
    packed, sent = pl.pallas_call(
        functools.partial(pack_kernel, first, parts),
        in_specs=[pl.BlockSpec(memory_space=pl.ANY)],
        out_specs=[pl.BlockSpec(memory_space=pl.ANY)] * 2,
        out_shape=[jax.ShapeDtypeStruct((devices, rows, columns), f32) for rows in (early, 2 * per_peer)],
        scratch_shapes=[
            pltpu.VMEM((2 * pairs, points, box_dev), f32),
            pltpu.VMEM((devices, pairs * per_peer, columns), f32),
            pltpu.SemaphoreType.DMA((parts,)),
            pltpu.SemaphoreType.DMA((2 * parts,)),
        ],
        compiler_params=params(),
        cost_estimate=cost(2, 6 << 20),
        name="pack_phases",
    )(turned)
    arrived = lax.all_to_all(packed, AXES, split_axis=0, concat_axis=0, tiled=True)

    whole = jax.ShapeDtypeStruct((box_dev, columns), f32)
    whole_spec = pl.BlockSpec((box_dev, columns), lambda k: (0, 0))
    state, last = pl.pallas_call(
        functools.partial(local_kernel, local),
        grid=(first // 2,),
        in_specs=[
            whole_spec,
            pl.BlockSpec((2, points, box_dev), lambda k: (k, 0, 0)),
            pl.BlockSpec((2, 2, 2, columns, columns), lambda k: (k, 0, 0, 0, 0)),
        ],
        out_specs=[whole_spec] * 2,
        out_shape=[whole] * 2,
        scratch_shapes=[pltpu.VMEM((box_dev, columns), f32)] * 2,
        compiler_params=params(),
        cost_estimate=cost(20, 18 << 20),
        name="local_levels",
    )(source, turned, interp_maps)

    wide = lax.axis_size("wide")
    partner = lax.ppermute(state, "wide", [(i, i ^ 1) for i in range(wide)])
    parity = jnp.reshape(lax.axis_index("wide") & 1, (1,)).astype(jnp.int32)
    sent = pl.pallas_call(
        core_kernel,
        grid_spec=pltpu.PrefetchScalarGridSpec(
            num_scalar_prefetch=1,
            grid=(4,),
            in_specs=[pl.BlockSpec((box_dev // 4, columns), lambda k, p: (k, 0))] * 3
            + [
                pl.BlockSpec((1, 1, 2, columns, columns), lambda k, p: (first - 1, p[0], 0, 0, 0)),
                pl.BlockSpec(memory_space=pl.ANY),
            ],
            out_specs=pl.BlockSpec((devices // 4, per_peer, columns), lambda k, p: (k, 0, 0)),
        ),
        out_shape=jax.ShapeDtypeStruct((devices, 2 * per_peer, columns), f32),
        input_output_aliases={5: 0},
        compiler_params=params(),
        cost_estimate=cost(3, 5 << 20),
        name="core_level",
    )(parity, state, partner, last, interp_maps, sent)

    weights = pl.pallas_call(
        maps_kernel,
        grid=(pairs,),
        in_specs=[pl.BlockSpec((2, 2, 2, columns, columns), lambda k: (first // 2 + k, 0, 0, 0, 0))],
        out_specs=pl.BlockSpec((2, 4 * columns, 2 * columns), lambda k: (k, 0, 0)),
        out_shape=jax.ShapeDtypeStruct((2 * pairs, 4 * columns, 2 * columns), jnp.bfloat16),
        compiler_params=params(),
        cost_estimate=cost(2, 3 << 20),
        name="last_maps",
    )(interp_maps)

    sent, arrived = lax.optimization_barrier((sent, arrived))
    final = lax.all_to_all(sent, AXES, split_axis=0, concat_axis=0, tiled=True)

    waves_shape = (2 * pairs - 2, 2, box_dev // 2, columns)
    waves = pl.pallas_call(
        functools.partial(angles_kernel, per_peer, pairs - 1),
        grid=(pairs - 1,),
        in_specs=[pl.BlockSpec((devices, per_peer, columns), lambda k: (0, k, 0))],
        out_specs=pl.BlockSpec((2, *waves_shape[1:]), lambda k: (k, 0, 0, 0)),
        out_shape=jax.ShapeDtypeStruct(waves_shape, f32),
        scratch_shapes=[pltpu.VMEM((box_dev, columns), f32)] * 2,
        compiler_params=params(),
        cost_estimate=cost(6, 9 << 20),
        name="angles",
    )(arrived)

    steps = box_dev // (2 * CHUNK)
    per_device_rows = pltpu.VMEM((devices, per_peer, columns), f32)
    rows = pltpu.VMEM((box_dev, columns), f32)
    out = pl.pallas_call(
        functools.partial(final_kernel, levels - first, per_peer),
        in_specs=[pl.BlockSpec(memory_space=pl.ANY)] * 3,
        out_specs=pl.BlockSpec(memory_space=pl.ANY),
        out_shape=jax.ShapeDtypeStruct((per_peer, devices, columns), f32),
        scratch_shapes=[
            per_device_rows,
            rows,
            per_device_rows,
            rows,
            rows,
            pltpu.VMEM((2 * pairs, *waves_shape[1:]), f32),
            pltpu.VMEM((2 * pairs, 4 * columns, 2 * columns), jnp.bfloat16),
            pltpu.VMEM((per_peer, devices, columns), f32),
            pltpu.SemaphoreType.DMA((4 * pairs + 2,)),
            pltpu.SemaphoreType.DMA((2 * steps,)),
        ],
        compiler_params=params(),
        cost_estimate=cost(6, 10 << 20),
        name="final_levels",
    )(final, waves, weights)
    return out.reshape(box_dev, columns)


def solution(mesh):
    in_specs = (P(AXES, None), P(), P(None, AXES, None))
    return jax.shard_map(per_device, mesh=mesh, in_specs=in_specs, out_specs=P(AXES, None), check_vma=False)
```

```python
import functools

import jax
import jax.numpy as jnp
from jax import lax
from jax.experimental import pallas as pl
from jax.experimental.pallas import tpu as pltpu
from jax.sharding import PartitionSpec as P

AXES = ("narrow", "wide")
SIN_HALF = (0.9999999957157406, -0.041666644924359314, 0.0005208156633383668, -3.095163447075199e-06, 1.0176428087056766e-08)
COS_HALF = (0.9999999532465265, -0.12499976265264102, 0.002603973680502671, -2.1646354078657635e-05, 9.044205735375736e-08)
CHUNK = 256
VMEM = 58 * 2**20


def horner(coefficients, z):
    total = jnp.full_like(z, coefficients[-1])
    for c in coefficients[-2::-1]:
        total = total * z + c
    return total


def cos_sin(x):
    z = x * x
    s = x * horner(SIN_HALF, z)
    c = horner(COS_HALF, z)
    return 1.0 - 0.5 * (s * s), s * c


def spread(cosine, sine, parity):
    left = lax.broadcasted_iota(jnp.int32, cosine.shape, 1) < 64
    c_roll = pltpu.roll(cosine, 64, 1)
    s_roll = pltpu.roll(sine, 64, 1)
    if parity == 0:
        return jnp.where(left, cosine, c_roll), jnp.where(left, -sine, s_roll)
    return jnp.where(left, c_roll, cosine), jnp.where(left, -s_roll, sine)


def rotate(values, cosine, sine, parity):
    c2, s2 = spread(cosine, sine, parity)
    return values * c2 + pltpu.roll(values, 64, 1) * s2


def dot3(x, w):
    upper = x.astype(jnp.bfloat16)
    lower = (x - upper.astype(jnp.float32)).astype(jnp.bfloat16)
    w = jnp.concatenate([w[: x.shape[1]], w], axis=0)
    return jnp.dot(jnp.concatenate([upper, lower, upper], axis=1), w, preferred_element_type=jnp.float32)


def row_slices(stride, step, n=CHUNK):
    if stride >= n:
        per = stride // n
        return [pl.ds((step // per) * 2 * stride + (step % per) * n, n)]
    base = step * 2 * n
    if stride >= 8:
        return [pl.ds(base + j * 2 * stride, stride) for j in range(n // stride)]
    return [pl.ds(base + o, n // stride, stride=2 * stride) for o in range(stride)]


def shifted(s, by):
    return pl.ds(s.start + by, s.size, stride=s.stride)


def load_pairs(ref, slices, stride):
    def cat(parts):
        return parts[0] if len(parts) == 1 else jnp.concatenate(parts, axis=0)

    return cat([ref[s, :] for s in slices]), cat([ref[shifted(s, stride), :] for s in slices])


def store_pairs(ref, slices, stride, low, high):
    at = 0
    for s in slices:
        ref[s, :] = low[at : at + s.size]
        ref[shifted(s, stride), :] = high[at : at + s.size]
        at += s.size


def pair_level(state, cosine, sine, w, stride, parity, put=None, ready=None):
    rows = state.shape[0]

    for i in range(rows // (2 * CHUNK)):
        if ready is not None:
            ready(i)
        slices = row_slices(stride, i)
        low, high = load_pairs(state, slices, stride)
        new = dot3(jnp.concatenate([low, high], axis=1), w)
        c_low, c_high = load_pairs(cosine, slices, stride)
        s_low, s_high = load_pairs(sine, slices, stride)
        low = rotate(new[:, :128], c_low, s_low, parity)
        high = rotate(new[:, 128:], c_high, s_high, parity)
        if put is None:
            store_pairs(state, slices, stride, low, high)
        else:
            put(i, low, high)


def pack_kernel(first, parts, phases, out, angles, packed, come, gone):
    levels, _, columns = angles.shape
    size = columns // parts
    devices = size // 16

    def arrive(i):
        at = pl.ds(i * size, size)
        return pltpu.make_async_copy(phases.at[pl.ds(first, levels), :, at], angles.at[:, :, at], come.at[i])

    def leave(i):
        at = pl.ds(i * devices, devices)
        return pltpu.make_async_copy(packed.at[at], out.at[at], gone.at[i])

    for i in range(parts):
        arrive(i).start()
    for i in range(parts):
        arrive(i).wait()
        for j in range(i * size // 128, (i + 1) * size // 128):
            for k in range(levels // 2):
                at = pl.ds(j * 128, 128)
                block = jnp.concatenate([angles[2 * k, :, at], angles[2 * k + 1, :, at]], axis=0)
                packed[pl.ds(j * 8, 8), pl.ds(k * 16, 16), :] = block.T.reshape(8, 16, 128)
        leave(i).start()
    for i in range(parts):
        leave(i).wait()


def halves(w):
    upper = w.astype(jnp.bfloat16)
    return jnp.concatenate([upper, (w - upper.astype(jnp.float32)).astype(jnp.bfloat16)], axis=0)


def split_map(maps):
    return halves(jnp.concatenate([jnp.concatenate([maps[0, i], maps[1, i]], axis=1) for i in range(2)], axis=0))


def split_map_planes(maps):
    real, imag = slice(0, 64), slice(64, 128)
    return halves(
        jnp.concatenate(
            [jnp.concatenate([maps[o, i][:, part] for part in (real, imag) for o in range(2)], axis=1) for i in range(2)], axis=0
        )
    )


def local_kernel(levels, source, phases, maps, state, cosine, sine):
    pair = pl.program_id(0)

    @pl.when(pair == 0)
    def _():
        state[...] = source[...]

    def angles(j, carry):
        at = pl.ds(pl.multiple_of(j * 128, 128), 128)
        block = jnp.concatenate([phases[0, :, at], phases[1, :, at]], axis=0)
        c, s = cos_sin(block.T)
        cosine[at, :] = c
        sine[at, :] = s
        return carry

    lax.fori_loop(0, phases.shape[2] // 128, angles, 0, unroll=True)
    for level in range(levels):

        @pl.when(pair == level // 2)
        def _():
            pair_level(state, cosine, sine, split_map(maps[level % 2]), 2**level, level % 2)


def core_kernel(parity_ref, own, partner, cosine, sine, maps, out):
    odd = parity_ref[0] == 1
    w = halves(jnp.concatenate([maps[0, 0, 0], maps[0, 0, 1]], axis=0))

    def step(i, carry):
        at = pl.ds(pl.multiple_of(i * CHUNK, CHUNK), CHUNK)
        mine, other = own[at, :], partner[at, :]
        low = jnp.where(odd, other, mine)
        high = jnp.where(odd, mine, other)
        new = dot3(jnp.concatenate([low, high], axis=1), w)
        out[at, :] = rotate(new, cosine[at, :], sine[at, :], 1)
        return carry

    lax.fori_loop(0, own.shape[0] // CHUNK, step, 0)


def angles_kernel(boxes, angles, maps, waves, weights, cos_rows, sin_rows):
    rows = cos_rows.shape[0]
    level = 2 * pl.program_id(0)
    c, s = cos_sin(angles[...].reshape(rows, 128))
    cos_rows[...] = c
    sin_rows[...] = s
    left = lax.broadcasted_iota(jnp.int32, (CHUNK, 128), 1) < 64
    for pair in range(3):

        @pl.when(pl.program_id(0) == pair)
        def _():
            for parity in range(2):
                stride = boxes * 2 ** (2 * pair + parity + 1)
                for i in range(rows // (2 * CHUNK)):
                    for which, here in enumerate((cos_rows, sin_rows)):
                        low, high = load_pairs(here, row_slices(stride, i), stride)
                        if parity == 0:
                            both = jnp.where(left, low, pltpu.roll(high, 64, 1))
                        else:
                            both = jnp.where(left, pltpu.roll(low, 64, 1), high)
                        waves[parity, which, pl.ds(i * CHUNK, CHUNK), :] = both

    for parity in range(2):
        weights[parity] = split_map_planes(maps[parity])


def plane_level(state, waves, w, stride, put=None):
    left = lax.broadcasted_iota(jnp.int32, (CHUNK, 128), 1) < 64
    for i in range(state.shape[0] // (2 * CHUNK)):
        slices = row_slices(stride, i)
        low, high = load_pairs(state, slices, stride)
        new = dot3(jnp.concatenate([low, high], axis=1), w)
        at = pl.ds(i * CHUNK, CHUNK)
        c, s = waves[0, at, :], waves[1, at, :]
        real, imag = new[:, :128], new[:, 128:]
        real, imag = real * c - imag * s, real * s + imag * c
        low = jnp.where(left, real, pltpu.roll(imag, 64, 1))
        high = jnp.where(left, pltpu.roll(real, 64, 1), imag)
        if put is None:
            store_pairs(state, slices, stride, low, high)
        else:
            put(i, low, high)


def final_kernel(levels, boxes, source, waves, weights, out, state, waves_here, w_here, turned, come, gone):
    steps = state.shape[0] // (2 * CHUNK)
    n = CHUNK // boxes
    half = out.shape[1] // 2

    def arrive(level):
        here = [
            pltpu.make_async_copy(weights.at[level], w_here.at[level], come.at[3 * level]),
            pltpu.make_async_copy(waves.at[level], waves_here.at[level], come.at[3 * level + 1]),
        ]
        return ([pltpu.make_async_copy(source, state, come.at[2])] if level == 0 else []) + here

    def leave(i, upper):
        at = pl.ds(upper * half + i * n, n)
        return pltpu.make_async_copy(turned.at[:, at, :], out.at[:, at, :], gone.at[2 * i + upper])

    def put(i, low, high):
        for upper, values in enumerate((low, high)):
            turned[:, pl.ds(upper * half + i * n, n), :] = jnp.swapaxes(values.reshape(n, boxes, 128), 0, 1)
            leave(i, upper).start()

    for level in range(levels):
        for copy in arrive(level):
            copy.start()
    groups = (0, 1, 3, 6)
    for level in range(levels):
        if level in groups:
            for other in range(level, groups[groups.index(level) + 1]):
                for copy in arrive(other):
                    copy.wait()
        plane_level(state, waves_here.at[level], w_here[level], boxes * 2 ** (level + 1), put if level == levels - 1 else None)
    for i in range(steps):
        leave(i, 0).wait()
        leave(i, 1).wait()


def params():
    return pltpu.CompilerParams(vmem_limit_bytes=VMEM)


def cost(microseconds, moved):
    return pl.CostEstimate(flops=int(microseconds * 1e9), bytes_accessed=moved, transcendentals=0)


def per_device(source, interp_maps, phases):
    box_dev, columns = source.shape
    f32 = jnp.float32
    devices = lax.axis_size("narrow") * lax.axis_size("wide")
    per_peer = box_dev // devices
    local = box_dev.bit_length() - 1
    levels = interp_maps.shape[0]
    first = local + 1
    pairs = (levels - first) // 2
    turned = jnp.transpose(phases, (0, 2, 1))
    points = turned.shape[1]

    parts = 4
    packed = pl.pallas_call(
        functools.partial(pack_kernel, first, parts),
        in_specs=[pl.BlockSpec(memory_space=pl.ANY)],
        out_specs=pl.BlockSpec(memory_space=pl.ANY),
        out_shape=jax.ShapeDtypeStruct((devices, pairs * per_peer, columns), f32),
        scratch_shapes=[
            pltpu.VMEM((2 * pairs, points, box_dev), f32),
            pltpu.VMEM((devices, pairs * per_peer, columns), f32),
            pltpu.SemaphoreType.DMA((parts,)),
            pltpu.SemaphoreType.DMA((parts,)),
        ],
        compiler_params=params(),
        cost_estimate=cost(2, 6 << 20),
        name="pack_phases",
    )(turned)
    arrived = lax.all_to_all(packed, AXES, split_axis=0, concat_axis=0, tiled=True)

    whole = jax.ShapeDtypeStruct((box_dev, columns), f32)
    whole_spec = pl.BlockSpec((box_dev, columns), lambda k: (0, 0))
    state, cosine, sine = pl.pallas_call(
        functools.partial(local_kernel, local),
        grid=(first // 2,),
        in_specs=[
            whole_spec,
            pl.BlockSpec((2, points, box_dev), lambda k: (k, 0, 0)),
            pl.BlockSpec((2, 2, 2, columns, columns), lambda k: (k, 0, 0, 0, 0)),
        ],
        out_specs=[whole_spec] * 3,
        out_shape=[whole] * 3,
        compiler_params=params(),
        cost_estimate=cost(20, 18 << 20),
        name="local_levels",
    )(source, turned, interp_maps)

    wide = lax.axis_size("wide")
    partner = lax.ppermute(state, "wide", [(i, i ^ 1) for i in range(wide)])
    parity = jnp.reshape(lax.axis_index("wide") & 1, (1,)).astype(jnp.int32)
    state = pl.pallas_call(
        core_kernel,
        grid_spec=pltpu.PrefetchScalarGridSpec(
            num_scalar_prefetch=1,
            grid=(4,),
            in_specs=[pl.BlockSpec((box_dev // 4, columns), lambda k, p: (k, 0))] * 4
            + [pl.BlockSpec((1, 1, 2, columns, columns), lambda k, p: (first - 1, p[0], 0, 0, 0))],
            out_specs=pl.BlockSpec((box_dev // 4, columns), lambda k, p: (k, 0)),
        ),
        out_shape=whole,
        compiler_params=params(),
        cost_estimate=cost(3, 5 << 20),
        name="core_level",
    )(parity, state, partner, cosine, sine, interp_maps)

    state, arrived = lax.optimization_barrier((state, arrived))
    state = lax.all_to_all(state.reshape(devices, per_peer, columns), AXES, split_axis=0, concat_axis=0, tiled=True)

    waves_shape = (2 * pairs, 2, box_dev // 2, columns)
    waves, weights = pl.pallas_call(
        functools.partial(angles_kernel, per_peer),
        grid=(pairs,),
        in_specs=[
            pl.BlockSpec((devices, per_peer, columns), lambda k: (0, k, 0)),
            pl.BlockSpec((2, 2, 2, columns, columns), lambda k: (first // 2 + k, 0, 0, 0, 0)),
        ],
        out_specs=[
            pl.BlockSpec((2, *waves_shape[1:]), lambda k: (k, 0, 0, 0)),
            pl.BlockSpec((2, 4 * columns, 2 * columns), lambda k: (k, 0, 0)),
        ],
        out_shape=[jax.ShapeDtypeStruct(waves_shape, f32), jax.ShapeDtypeStruct((2 * pairs, 4 * columns, 2 * columns), jnp.bfloat16)],
        scratch_shapes=[pltpu.VMEM((box_dev, columns), f32)] * 2,
        compiler_params=params(),
        cost_estimate=cost(6, 9 << 20),
        name="angles",
    )(arrived, interp_maps)

    steps = box_dev // (2 * CHUNK)
    out = pl.pallas_call(
        functools.partial(final_kernel, levels - first, per_peer),
        in_specs=[pl.BlockSpec(memory_space=pl.ANY)] * 3,
        out_specs=pl.BlockSpec(memory_space=pl.ANY),
        out_shape=jax.ShapeDtypeStruct((per_peer, devices, columns), f32),
        scratch_shapes=[
            pltpu.VMEM((box_dev, columns), f32),
            pltpu.VMEM(waves_shape, f32),
            pltpu.VMEM((2 * pairs, 4 * columns, 2 * columns), jnp.bfloat16),
            pltpu.VMEM((per_peer, devices, columns), f32),
            pltpu.SemaphoreType.DMA((6 * pairs,)),
            pltpu.SemaphoreType.DMA((2 * steps,)),
        ],
        compiler_params=params(),
        cost_estimate=cost(6, 10 << 20),
        name="final_levels",
    )(state.reshape(box_dev, columns), waves, weights)
    return out.reshape(box_dev, columns)


def solution(mesh):
    in_specs = (P(AXES, None), P(), P(None, AXES, None))
    return jax.shard_map(per_device, mesh=mesh, in_specs=in_specs, out_specs=P(AXES, None), check_vma=False)
```
